32 devices in a mesh: row: 4 (over y, x), col: 8 (over z, core).
Axes of the slice: x: 2, y: 2, z: 4, core: 2. Of those that a mesh axis runs over, the one named last changes fastest.
Arguments:
- features: bfloat16 [32768, 128], P(('col', 'row')), may hold values from -6 to 6
- tiles: bfloat16 [4, 8, 512, 128, 128], P('row', 'col'), may hold values from -0.21875 to 0.21875
- tile_rows: int32 [4, 8, 512], P('row', 'col'), may hold values from 0 to 63
- tile_cols: int32 [4, 8, 512], P('row', 'col'), may hold values from 0 to 31
- tile_counts: int32 [4, 8], P('row', 'col'), may hold values from 128 to 512, as said below
- weight: bfloat16 [128, 128], replicated, may hold values from -0.5 to 0.5
- bias: float32 [128], replicated, may hold values from -3 to 3
Outputs:
- hidden: bfloat16 [32768, 128], P(('row', 'col'))
The draws below stay inside these ranges and needn't reach their ends.
Inputs may be any that keep to these rules, and one draw needn't show every extreme that they name: `tile_counts`: some grid cell has exactly 512 live slots in every draw.
All inputs are finite; a program needn't handle non-finite values.
Results may differ from the reference program's by a relative error of at most 0.014.
Values may be sent and summed in bfloat16 or wider, within the bound.
A program may use at most 192 MiB of HBM per device.

```python
import jax
import jax.numpy as jnp
from jax import lax

F = 128
OWN = 1024
TILES = 512
NODES = 32768
RB = 64
CB = 32
N_ROW = 4
N_COL = 8


def draw_tile_counts(key, part):
    key = jax.random.fold_in(key, 7)
    first = jax.random.fold_in(key, 1)
    second = jax.random.fold_in(key, 2)
    counts = jax.random.randint(first, (N_ROW * N_COL,), TILES // 4, TILES + 1)
    chosen = jax.random.randint(second, (), 0, N_ROW * N_COL)
    counts = counts.at[chosen].set(TILES)
    return counts.reshape(N_ROW, N_COL).astype(jnp.int32)


def place_ends(array, rng, low, largest):
    shape = array.shape
    spot = [jax.random.randint(jax.random.fold_in(rng, axis), (), 0, shape[axis]) for axis in range(len(shape))]
    array = array.at[tuple(spot)].set(low)
    longest = shape.index(max(shape))
    spot[longest] = (spot[longest] + 1) % shape[longest]
    return array.at[tuple(spot)].set(largest)


def shard_levels(own_key, extent, cuts, least, top_value):
    def one(position, parts):
        draws = jax.random.uniform(jax.random.fold_in(jax.random.fold_in(own_key, 6), position), (parts,), jnp.float32, least / len(cuts), top_value / len(cuts))
        return jnp.repeat(jnp.exp(draws), extent[position] // parts).reshape((-1,) + (1,) * (len(extent) - position - 1))

    level = one(*cuts[0])
    for cut in cuts[1:]:
        level = level * one(*cut)
    return level


def normal_values(key, dims, width, most, pieces=(), held_as=jnp.bfloat16):
    level = shard_levels(key, dims, pieces, -0.22, 0.18) if pieces else 1.0
    result = jax.random.normal(key, dims, jnp.float32) * width * level
    return jnp.minimum(jnp.maximum(result, -most), most).astype(held_as)


def setup_inputs(seed: int = 0) -> dict:
    keys = jax.random.split(jax.random.key(seed), 8)
    return {
        "features": normal_values(keys[0], (NODES, F), 1.0, 6.0, ((0, 32),)),
        "tiles": normal_values(keys[1], (N_ROW, N_COL, TILES, 128, 128), ((10240.0 * TILES / OWN) ** -0.5), 0.21875, ((0, 4), (1, 8))),
        "tile_rows": place_ends(jax.random.randint(keys[2], (N_ROW, N_COL, TILES), 0, RB), jax.random.fold_in(keys[2], 1), 0, RB - 1).astype(jnp.int32),
        "tile_cols": place_ends(jax.random.randint(keys[3], (N_ROW, N_COL, TILES), 0, CB), jax.random.fold_in(keys[3], 1), 0, CB - 1).astype(jnp.int32),
        "tile_counts": draw_tile_counts(jax.random.fold_in(keys[7], 71), 0),
        "weight": normal_values(keys[5], (F, F), F ** -0.5, 0.5),
        "bias": normal_values(keys[6], (F,), 0.5, 3.0, (), jnp.float32),
    }


def reference(features, tiles, tile_rows, tile_cols, tile_counts, weight, bias):
    blocks_x = features.reshape(NODES // 128, 128, F)
    total = jnp.zeros((N_ROW, RB, 128, F), jnp.float32)
    slots = jnp.arange(TILES, dtype=jnp.int32)

    def step(acc, index):
        r = index // N_COL
        c = index % N_COL
        cell = tiles[r, c].astype(jnp.float32)
        rows = tile_rows[r, c].astype(jnp.int32)
        cols = (c * CB + tile_cols[r, c]).astype(jnp.int32)
        picked = blocks_x[cols].astype(jnp.float32)
        prod = jnp.einsum("tij,tjf->tif", cell, picked)
        live = (slots < tile_counts[r, c]).astype(jnp.float32)
        prod = prod * live[:, None, None]
        partial_value = jnp.zeros((RB, 128, F), jnp.float32).at[rows].add(prod)
        partial_value = partial_value.astype(jnp.bfloat16).astype(jnp.float32)
        band_now = lax.dynamic_index_in_dim(acc, r, 0, keepdims=False)
        return lax.dynamic_update_index_in_dim(acc, band_now + partial_value, r, 0), None

    total, unused = lax.scan(step, total, jnp.arange(N_ROW * N_COL, dtype=jnp.int32))
    aggregated = total.reshape(NODES, F).astype(jnp.bfloat16)
    mixed = jnp.dot(aggregated, weight, preferred_element_type=jnp.float32) + bias
    return jnp.maximum(mixed, 0.0).astype(jnp.bfloat16)
```

```python
import functools

import jax
import jax.numpy as jnp
from jax import lax
from jax.experimental import pallas as pl
from jax.experimental.pallas import tpu as pltpu
from jax.sharding import PartitionSpec as P

MESH = pl.DeviceIdType.MESH
BLK = 128
GROUP = 16
CHUNK = 32
PIECES = 2


def gather_kernel(n_row, feat_ref, band_ref, send_sem, recv_sem, own_sem):
    me = lax.axis_index("row")
    own = feat_ref.shape[0]
    barrier = pltpu.get_barrier_semaphore()
    for k in range(1, n_row):
        peer = lax.rem(me + k, n_row)
        pl.semaphore_signal(barrier, inc=1, device_id={"row": peer}, device_id_type=MESH)
    pl.semaphore_wait(barrier, n_row - 1)
    slot = pl.ds(pl.multiple_of(me * own, own), own)
    copies = []
    for k in range(1, n_row):
        peer = lax.rem(me + k, n_row)
        copy = pltpu.make_async_remote_copy(
            src_ref=feat_ref,
            dst_ref=band_ref.at[slot],
            send_sem=send_sem.at[k],
            recv_sem=recv_sem.at[k],
            device_id={"row": peer},
            device_id_type=MESH,
        )
        copy.start()
        copies.append(copy)
    local_copy = pltpu.make_async_copy(feat_ref, band_ref.at[slot], own_sem)
    local_copy.start()
    local_copy.wait()
    for k in range(1, n_row):
        src = lax.rem(me - k + n_row, n_row)
        src_slot = pl.ds(pl.multiple_of(src * own, own), own)
        copies[k - 1].wait_send()
        pltpu.make_async_remote_copy(
            src_ref=feat_ref,
            dst_ref=band_ref.at[src_slot],
            send_sem=send_sem.at[k],
            recv_sem=recv_sem.at[k],
            device_id={"row": src},
            device_id_type=MESH,
        ).wait_recv()


def gather(features, n_row):
    own, width = features.shape
    return pl.pallas_call(
        functools.partial(gather_kernel, n_row),
        out_shape=jax.ShapeDtypeStruct((n_row * own, width), features.dtype),
        in_specs=[pl.BlockSpec(memory_space=pl.ANY)],
        out_specs=pl.BlockSpec(memory_space=pl.ANY),
        scratch_shapes=[
            pltpu.SemaphoreType.DMA((n_row,)),
            pltpu.SemaphoreType.DMA((n_row,)),
            pltpu.SemaphoreType.DMA,
        ],
        compiler_params=pltpu.CompilerParams(collective_id=0, has_side_effects=True),
        name="gather_band",
    )(features)


def cell_kernel(slots, row_blocks, rows_ref, cols_ref, count_ref, band_ref, tiles_ref, out_ref, held, acc, sem):
    count = count_ref[0]
    chunks = slots // CHUNK

    def chunk_copy(i):
        part = pl.ds(i * CHUNK, CHUNK)
        return pltpu.make_async_copy(tiles_ref.at[part], held.at[part], sem.at[i])

    for i in range(chunks):
        @pl.when(i * CHUNK < count)
        def _():
            chunk_copy(i).start()

    def clear(i, carry):
        acc[i] = jnp.zeros(acc.shape[1:], acc.dtype)
        return carry

    lax.fori_loop(0, row_blocks + 1, clear, 0, unroll=False)

    def group(g, carry):
        base = g * GROUP

        @pl.when(lax.rem(base, CHUNK) == 0)
        def _():
            chunk_copy(lax.div(base, CHUNK)).wait()

        for u in range(GROUP):
            t = base + u
            row = jnp.where(t < count, rows_ref[t], row_blocks)
            block = band_ref[cols_ref[t]]
            acc[row] += jnp.dot(held[t], block, preferred_element_type=jnp.float32)
        return carry

    lax.fori_loop(0, lax.div(count + GROUP - 1, GROUP), group, 0)

    def emit(i, carry):
        out_ref[i] = acc[i].astype(out_ref.dtype)
        return carry

    lax.fori_loop(0, row_blocks, emit, 0)


def cell_partial(rows, cols, count, band, tiles, row_blocks):
    slots = tiles.shape[0]
    width = band.shape[1]
    col_blocks = band.shape[0] // BLK
    smem = pl.BlockSpec(memory_space=pltpu.SMEM)
    vmem = pl.BlockSpec(memory_space=pltpu.VMEM)
    return pl.pallas_call(
        functools.partial(cell_kernel, slots, row_blocks),
        out_shape=jax.ShapeDtypeStruct((row_blocks, BLK, width), jnp.bfloat16),
        in_specs=[smem, smem, smem, vmem, pl.BlockSpec(memory_space=pl.ANY)],
        out_specs=vmem,
        scratch_shapes=[
            pltpu.VMEM((slots, BLK, BLK), jnp.bfloat16),
            pltpu.VMEM((row_blocks + 1, BLK, width), jnp.float32),
            pltpu.SemaphoreType.DMA((slots // CHUNK,)),
        ],
        compiler_params=pltpu.CompilerParams(vmem_limit_bytes=48 * 1024 * 1024),
        cost_estimate=pl.CostEstimate(
            flops=2 * slots * BLK * BLK * width, bytes_accessed=slots * BLK * BLK * 2, transcendentals=0
        ),
        name="cell_partial",
    )(rows, cols, count, band.reshape(col_blocks, BLK, width), tiles)


def reduce_kernel(
    line, own, part_ref, weight_ref, bias_ref, out_ref,
    pair_buf, up_in, down_in, up_out, down_out,
    pair_send, pair_recv, up_send, up_recv, down_send, down_recv,
):
    col = lax.axis_index("col")
    chip = lax.div(col, 2)
    core = lax.rem(col, 2)
    other = 1 - core
    rows = own // PIECES
    f32 = jnp.float32
    has_low = chip > 0
    has_high = chip < line - 1
    partner = chip * 2 + other
    high = lax.rem(col + 2, 2 * line)
    low = lax.rem(col - 2 + 2 * line, 2 * line)

    barrier = pltpu.get_barrier_semaphore()
    pl.semaphore_signal(barrier, inc=1, device_id={"col": partner}, device_id_type=MESH)

    @pl.when(has_low)
    def _():
        pl.semaphore_signal(barrier, inc=1, device_id={"col": low}, device_id_type=MESH)

    @pl.when(has_high)
    def _():
        pl.semaphore_signal(barrier, inc=1, device_id={"col": high}, device_id_type=MESH)

    pl.semaphore_wait(barrier, 1 + jnp.where(has_low, 1, 0) + jnp.where(has_high, 1, 0))

    def pair_copy(dest):
        start = pl.multiple_of((dest * 2 + other) * own, own)
        return pltpu.make_async_remote_copy(
            src_ref=part_ref.at[pl.ds(start, own)],
            dst_ref=pair_buf.at[dest],
            send_sem=pair_send.at[dest],
            recv_sem=pair_recv.at[dest],
            device_id={"col": partner},
            device_id_type=MESH,
        )

    def line_copy(dest, piece, upward):
        span = pl.ds(piece * rows, rows)
        src, dst = (up_out, up_in) if upward else (down_out, down_in)
        send, recv = (up_send, up_recv) if upward else (down_send, down_recv)
        return pltpu.make_async_remote_copy(
            src_ref=src.at[dest, span],
            dst_ref=dst.at[dest, span],
            send_sem=send.at[dest, piece],
            recv_sem=recv.at[dest, piece],
            device_id={"col": high if upward else low},
            device_id_type=MESH,
        )

    def pair_sum(dest, piece):
        mine = pl.ds(pl.multiple_of((dest * 2 + core) * own + piece * rows, rows), rows)
        span = pl.ds(piece * rows, rows)
        return part_ref[mine, :].astype(f32) + pair_buf[dest, span, :].astype(f32)

    for dist in range(line - 1, 0, -1):
        @pl.when(chip + dist < line)
        def _():
            pair_copy(chip + dist).start()

        @pl.when(chip - dist >= 0)
        def _():
            pair_copy(chip - dist).start()

    pair_copy(chip).start()

    def forward(dest, piece, upward):
        if piece == 0:
            pair_copy(dest).wait_recv()
        from_line = has_low if upward else has_high
        buf = up_in if upward else down_in
        out = up_out if upward else down_out
        span = pl.ds(piece * rows, rows)

        @pl.when(from_line)
        def _():
            line_copy(dest, piece, upward).wait_recv()
            out[dest, span, :] = (pair_sum(dest, piece) + buf[dest, span, :].astype(f32)).astype(out.dtype)

        @pl.when(jnp.logical_not(from_line))
        def _():
            out[dest, span, :] = pair_sum(dest, piece).astype(out.dtype)

        line_copy(dest, piece, upward).start()

    for dist in range(line - 1, 0, -1):
        for piece in range(PIECES):
            @pl.when(chip + dist < line)
            def _():
                forward(chip + dist, piece, True)

            @pl.when(chip - dist >= 0)
            def _():
                forward(chip - dist, piece, False)

    pair_copy(chip).wait_recv()
    for piece in range(PIECES):
        span = pl.ds(piece * rows, rows)

        @pl.when(has_low)
        def _():
            line_copy(chip, piece, True).wait_recv()

        @pl.when(has_high)
        def _():
            line_copy(chip, piece, False).wait_recv()

        total = pair_sum(chip, piece)
        total = total + jnp.where(has_low, up_in[chip, span, :].astype(f32), 0.0)
        total = total + jnp.where(has_high, down_in[chip, span, :].astype(f32), 0.0)
        mixed = jnp.dot(total.astype(jnp.bfloat16), weight_ref[...], preferred_element_type=f32)
        out_ref[span, :] = jnp.maximum(mixed + bias_ref[...], 0.0).astype(out_ref.dtype)

    for dest in range(line):
        pair_copy(dest).wait_send()
        for piece in range(PIECES):
            @pl.when(chip < dest)
            def _():
                line_copy(dest, piece, True).wait_send()

            @pl.when(chip > dest)
            def _():
                line_copy(dest, piece, False).wait_send()


def reduce_mix(partial_value, weight, bias, n_col, own):
    width = partial_value.shape[1]
    line = n_col // 2
    vmem = pl.BlockSpec(memory_space=pltpu.VMEM)
    buf = pltpu.VMEM((line, own, width), jnp.bfloat16)
    sems = pltpu.SemaphoreType.DMA((line, PIECES))
    pair_sems = pltpu.SemaphoreType.DMA((line,))
    return pl.pallas_call(
        functools.partial(reduce_kernel, line, own),
        out_shape=jax.ShapeDtypeStruct((own, width), jnp.bfloat16),
        in_specs=[vmem, vmem, vmem],
        out_specs=vmem,
        scratch_shapes=[buf, buf, buf, buf, buf, pair_sems, pair_sems, sems, sems, sems, sems],
        compiler_params=pltpu.CompilerParams(
            collective_id=1, has_side_effects=True, vmem_limit_bytes=48 * 1024 * 1024
        ),
        name="reduce_mix",
    )(partial_value, weight, bias)


def local(n_row, n_col, features, tiles, tile_rows, tile_cols, tile_counts, weight, bias):
    own, width = features.shape
    slots = tiles.shape[2]
    band = gather(features, n_row)
    row_blocks = n_col * own // BLK
    partial_value = cell_partial(
        tile_rows.reshape(slots),
        tile_cols.reshape(slots),
        tile_counts.reshape(1),
        band,
        tiles.reshape(slots, BLK, BLK),
        row_blocks,
    )
    return reduce_mix(
        partial_value.reshape(row_blocks * BLK, width), weight, bias.reshape(1, width), n_col, own
    )


def solution(mesh):
    in_specs = (
        P(("col", "row"), None),
        P("row", "col", None, None, None),
        P("row", "col", None),
        P("row", "col", None),
        P("row", "col"),
        P(),
        P(),
    )
    out_specs = P(("row", "col"), None)
    fn = functools.partial(local, mesh.shape["row"], mesh.shape["col"])
    return jax.shard_map(fn, mesh=mesh, in_specs=in_specs, out_specs=out_specs, check_vma=False)
```

```python
import functools

import jax
import jax.numpy as jnp
from jax import lax
from jax.experimental import pallas as pl
from jax.experimental.pallas import tpu as pltpu
from jax.sharding import PartitionSpec as P

MESH = pl.DeviceIdType.MESH
BLK = 128
CHUNK = 32
PIECES = 4


def gather_kernel(n_row, feat_ref, band_ref, send_sem, recv_sem, own_sem):
    me = lax.axis_index("row")
    own = feat_ref.shape[0]
    barrier = pltpu.get_barrier_semaphore()
    for k in range(1, n_row):
        peer = lax.rem(me + k, n_row)
        pl.semaphore_signal(barrier, inc=1, device_id={"row": peer}, device_id_type=MESH)
    pl.semaphore_wait(barrier, n_row - 1)
    slot = pl.ds(pl.multiple_of(me * own, own), own)
    copies = []
    for k in range(1, n_row):
        peer = lax.rem(me + k, n_row)
        copy = pltpu.make_async_remote_copy(
            src_ref=feat_ref,
            dst_ref=band_ref.at[slot],
            send_sem=send_sem.at[k],
            recv_sem=recv_sem.at[k],
            device_id={"row": peer},
            device_id_type=MESH,
        )
        copy.start()
        copies.append(copy)
    local_copy = pltpu.make_async_copy(feat_ref, band_ref.at[slot], own_sem)
    local_copy.start()
    local_copy.wait()
    for k in range(1, n_row):
        src = lax.rem(me - k + n_row, n_row)
        src_slot = pl.ds(pl.multiple_of(src * own, own), own)
        copies[k - 1].wait_send()
        pltpu.make_async_remote_copy(
            src_ref=feat_ref,
            dst_ref=band_ref.at[src_slot],
            send_sem=send_sem.at[k],
            recv_sem=recv_sem.at[k],
            device_id={"row": src},
            device_id_type=MESH,
        ).wait_recv()


def relay_kernel(feat_ref, band_ref, send_sem, recv_sem, own_sem):
    me = lax.axis_index("row")
    own = feat_ref.shape[0]
    half = own // 2
    slow, fast = lax.div(me, 2), lax.rem(me, 2)
    peers = (slow * 2 + (1 - fast), (1 - slow) * 2 + fast)
    opposite = (1 - slow) * 2 + (1 - fast)
    barrier = pltpu.get_barrier_semaphore()
    for peer in peers:
        pl.semaphore_signal(barrier, inc=1, device_id={"row": peer}, device_id_type=MESH)
    local_copy = pltpu.make_async_copy(feat_ref, band_ref.at[pl.ds(pl.multiple_of(me * own, own), own)], own_sem)
    local_copy.start()
    pl.semaphore_wait(barrier, 2)

    def span(owner, part):
        return pl.ds(pl.multiple_of(owner * own + part * half, half), half)

    def copy(axis, step, source, owner, part):
        return pltpu.make_async_remote_copy(
            src_ref=source,
            dst_ref=band_ref.at[span(owner, part)],
            send_sem=send_sem.at[axis, step],
            recv_sem=recv_sem.at[axis, step],
            device_id={"row": peers[axis]},
            device_id_type=MESH,
        )

    def own_part(part):
        return feat_ref.at[pl.ds(part * half, half)]

    for step in range(2):
        for axis in range(2):
            part = axis if step == 0 else 1 - axis
            copy(axis, step, own_part(part), me, part).start()
    for axis in range(2):
        copy(axis, 0, own_part(axis), peers[axis], axis).wait_recv()
        copy(1 - axis, 2, band_ref.at[span(peers[axis], axis)], peers[axis], axis).start()
    local_copy.wait()
    for axis in range(2):
        copy(axis, 1, own_part(0), peers[axis], 1 - axis).wait_recv()
    for axis in range(2):
        copy(axis, 2, own_part(0), opposite, 1 - axis).wait_recv()
    for axis in range(2):
        for step in range(3):
            copy(axis, step, own_part(0), me, 0).wait_send()


def gather(features, n_row):
    own, width = features.shape
    if n_row == 4:
        kernel, sem_shape = relay_kernel, (2, 3)
    else:
        kernel, sem_shape = functools.partial(gather_kernel, n_row), (n_row,)
    return pl.pallas_call(
        kernel,
        out_shape=jax.ShapeDtypeStruct((n_row * own, width), features.dtype),
        in_specs=[pl.BlockSpec(memory_space=pl.ANY)],
        out_specs=pl.BlockSpec(memory_space=pltpu.VMEM),
        scratch_shapes=[
            pltpu.SemaphoreType.DMA(sem_shape),
            pltpu.SemaphoreType.DMA(sem_shape),
            pltpu.SemaphoreType.DMA,
        ],
        compiler_params=pltpu.CompilerParams(
            collective_id=0, has_side_effects=True, vmem_limit_bytes=16 * 1024 * 1024
        ),
        name="gather_band",
    )(features)


def cell_kernel(
    slots, row_blocks, rows_hbm, cols_hbm, count_ref, band_ref, tiles_ref, out_ref,
    rows_ref, cols_ref, held, acc, sem, index_sem,
):
    count = count_ref[0]
    chunks = slots // CHUNK

    def chunk_copy(i):
        part = pl.ds(i * CHUNK, CHUNK)
        return pltpu.make_async_copy(tiles_ref.at[part], held.at[part], sem.at[i])

    rows_copy = pltpu.make_async_copy(rows_hbm, rows_ref, index_sem.at[0])
    cols_copy = pltpu.make_async_copy(cols_hbm, cols_ref, index_sem.at[1])
    rows_copy.start()
    cols_copy.start()
    for i in range(chunks):
        @pl.when(i * CHUNK < count)
        def _():
            chunk_copy(i).start()

    def clear(i, carry):
        acc[i] = jnp.zeros(acc.shape[1:], acc.dtype)
        return carry

    lax.fori_loop(0, row_blocks, clear, 0, unroll=8)
    rows_copy.wait()
    cols_copy.wait()

    def chunk_step(i, carry):
        chunk_copy(i).wait()
        for u in range(CHUNK):
            t = i * CHUNK + u
            row = jnp.where(t < count, rows_ref[t], row_blocks)
            block = band_ref[cols_ref[t]]
            acc[row] += jnp.dot(held[t], block, preferred_element_type=jnp.float32)
        return carry

    lax.fori_loop(0, lax.div(count + CHUNK - 1, CHUNK), chunk_step, 0)

    def emit(i, carry):
        out_ref[i] = acc[i].astype(out_ref.dtype)
        return carry

    lax.fori_loop(0, row_blocks, emit, 0, unroll=8)


def cell_partial(rows, cols, count, band, tiles, row_blocks):
    slots = tiles.shape[0]
    width = band.shape[1]
    col_blocks = band.shape[0] // BLK
    smem = pl.BlockSpec(memory_space=pltpu.SMEM)
    hbm = pl.BlockSpec(memory_space=pl.ANY)
    vmem = pl.BlockSpec(memory_space=pltpu.VMEM)
    return pl.pallas_call(
        functools.partial(cell_kernel, slots, row_blocks),
        out_shape=jax.ShapeDtypeStruct((row_blocks, BLK, width), jnp.bfloat16),
        in_specs=[hbm, hbm, smem, vmem, hbm],
        out_specs=vmem,
        scratch_shapes=[
            pltpu.SMEM((slots,), jnp.int32),
            pltpu.SMEM((slots,), jnp.int32),
            pltpu.VMEM((slots, BLK, BLK), jnp.bfloat16),
            pltpu.VMEM((row_blocks + 1, BLK, width), jnp.float32),
            pltpu.SemaphoreType.DMA((slots // CHUNK,)),
            pltpu.SemaphoreType.DMA((2,)),
        ],
        compiler_params=pltpu.CompilerParams(vmem_limit_bytes=48 * 1024 * 1024),
        cost_estimate=pl.CostEstimate(
            flops=2 * slots * BLK * BLK * width, bytes_accessed=slots * BLK * BLK * 2, transcendentals=0
        ),
        name="cell_partial",
    )(rows, cols, count, band.reshape(col_blocks, BLK, width), tiles)


def reduce_kernel(
    line, own, part_ref, weight_ref, bias_ref, out_ref,
    pair_buf, up_in, down_in, up_out, down_out,
    pair_send, pair_recv, up_send, up_recv, down_send, down_recv,
):
    col = lax.axis_index("col")
    chip = lax.div(col, 2)
    core = lax.rem(col, 2)
    other = 1 - core
    rows = own // PIECES
    f32 = jnp.float32
    has_low = chip > 0
    has_high = chip < line - 1
    partner = chip * 2 + other
    high = lax.rem(col + 2, 2 * line)
    low = lax.rem(col - 2 + 2 * line, 2 * line)

    barrier = pltpu.get_barrier_semaphore()
    pl.semaphore_signal(barrier, inc=1, device_id={"col": partner}, device_id_type=MESH)

    @pl.when(has_low)
    def _():
        pl.semaphore_signal(barrier, inc=1, device_id={"col": low}, device_id_type=MESH)

    @pl.when(has_high)
    def _():
        pl.semaphore_signal(barrier, inc=1, device_id={"col": high}, device_id_type=MESH)

    pl.semaphore_wait(barrier, 1 + jnp.where(has_low, 1, 0) + jnp.where(has_high, 1, 0))

    def pair_copy(dest):
        start = pl.multiple_of((dest * 2 + other) * own, own)
        return pltpu.make_async_remote_copy(
            src_ref=part_ref.at[pl.ds(start, own)],
            dst_ref=pair_buf.at[dest],
            send_sem=pair_send.at[dest],
            recv_sem=pair_recv.at[dest],
            device_id={"col": partner},
            device_id_type=MESH,
        )

    def line_copy(dest, piece, upward):
        span = pl.ds(piece * rows, rows)
        src, dst = (up_out, up_in) if upward else (down_out, down_in)
        send, recv = (up_send, up_recv) if upward else (down_send, down_recv)
        return pltpu.make_async_remote_copy(
            src_ref=src.at[dest, span],
            dst_ref=dst.at[dest, span],
            send_sem=send.at[dest, piece],
            recv_sem=recv.at[dest, piece],
            device_id={"col": high if upward else low},
            device_id_type=MESH,
        )

    def pair_sum(dest, piece):
        mine = pl.ds(pl.multiple_of((dest * 2 + core) * own + piece * rows, rows), rows)
        span = pl.ds(piece * rows, rows)
        return part_ref[mine, :].astype(f32) + pair_buf[dest, span, :].astype(f32)

    for dist in range(line - 1, 0, -1):
        @pl.when(chip + dist < line)
        def _():
            pair_copy(chip + dist).start()

        @pl.when(chip - dist >= 0)
        def _():
            pair_copy(chip - dist).start()

    pair_copy(chip).start()

    def forward(dest, piece, upward):
        if piece == 0:
            pair_copy(dest).wait_recv()
        from_line = has_low if upward else has_high
        buf = up_in if upward else down_in
        out = up_out if upward else down_out
        span = pl.ds(piece * rows, rows)

        @pl.when(from_line)
        def _():
            line_copy(dest, piece, upward).wait_recv()
            out[dest, span, :] = (pair_sum(dest, piece) + buf[dest, span, :].astype(f32)).astype(out.dtype)

        @pl.when(jnp.logical_not(from_line))
        def _():
            out[dest, span, :] = pair_sum(dest, piece).astype(out.dtype)

        line_copy(dest, piece, upward).start()

    for dist in range(line - 1, 0, -1):
        for piece in range(PIECES):
            @pl.when(chip + dist < line)
            def _():
                forward(chip + dist, piece, True)

            @pl.when(chip - dist >= 0)
            def _():
                forward(chip - dist, piece, False)

    pair_copy(chip).wait_recv()
    for piece in range(PIECES):
        span = pl.ds(piece * rows, rows)

        @pl.when(has_low)
        def _():
            line_copy(chip, piece, True).wait_recv()

        @pl.when(has_high)
        def _():
            line_copy(chip, piece, False).wait_recv()

        total = pair_sum(chip, piece)
        total = total + jnp.where(has_low, up_in[chip, span, :].astype(f32), 0.0)
        total = total + jnp.where(has_high, down_in[chip, span, :].astype(f32), 0.0)
        mixed = jnp.dot(total.astype(jnp.bfloat16), weight_ref[...], preferred_element_type=f32)
        out_ref[span, :] = jnp.maximum(mixed + bias_ref[...], 0.0).astype(out_ref.dtype)

    for dest in range(line):
        pair_copy(dest).wait_send()
        for piece in range(PIECES):
            @pl.when(chip < dest)
            def _():
                line_copy(dest, piece, True).wait_send()

            @pl.when(chip > dest)
            def _():
                line_copy(dest, piece, False).wait_send()


def reduce_mix(partial_value, weight, bias, n_col, own):
    width = partial_value.shape[1]
    line = n_col // 2
    vmem = pl.BlockSpec(memory_space=pltpu.VMEM)
    buf = pltpu.VMEM((line, own, width), jnp.bfloat16)
    sems = pltpu.SemaphoreType.DMA((line, PIECES))
    pair_sems = pltpu.SemaphoreType.DMA((line,))
    return pl.pallas_call(
        functools.partial(reduce_kernel, line, own),
        out_shape=jax.ShapeDtypeStruct((own, width), jnp.bfloat16),
        in_specs=[vmem, vmem, vmem],
        out_specs=vmem,
        scratch_shapes=[buf, buf, buf, buf, buf, pair_sems, pair_sems, sems, sems, sems, sems],
        compiler_params=pltpu.CompilerParams(
            collective_id=1, has_side_effects=True, vmem_limit_bytes=48 * 1024 * 1024
        ),
        name="reduce_mix",
    )(partial_value, weight, bias)


def local(n_row, n_col, features, tiles, tile_rows, tile_cols, tile_counts, weight, bias):
    own, width = features.shape
    slots = tiles.shape[2]
    band = gather(features, n_row)
    row_blocks = n_col * own // BLK
    partial_value = cell_partial(
        tile_rows.reshape(slots),
        tile_cols.reshape(slots),
        tile_counts.reshape(1),
        band,
        tiles.reshape(slots, BLK, BLK),
        row_blocks,
    )
    return reduce_mix(
        partial_value.reshape(row_blocks * BLK, width), weight, bias.reshape(1, width), n_col, own
    )


def solution(mesh):
    in_specs = (
        P(("col", "row"), None),
        P("row", "col", None, None, None),
        P("row", "col", None),
        P("row", "col", None),
        P("row", "col"),
        P(),
        P(),
    )
    out_specs = P(("row", "col"), None)
    fn = functools.partial(local, mesh.shape["row"], mesh.shape["col"])
    return jax.shard_map(fn, mesh=mesh, in_specs=in_specs, out_specs=out_specs, check_vma=False)
```

```python
import functools

import jax
import jax.numpy as jnp
from jax import lax
from jax.experimental import pallas as pl
from jax.experimental.pallas import tpu as pltpu
from jax.sharding import PartitionSpec as P

MESH = pl.DeviceIdType.MESH
BLK = 128
CHUNK = 64
PIECES = 4


def fill_zero(total_ref):
    def fill(i, carry):
        total_ref[i] = jnp.zeros(total_ref.shape[1:], total_ref.dtype)
        return carry

    lax.fori_loop(0, total_ref.shape[0], fill, 0)


def gather_kernel(n_row, feat_ref, band_ref, total_ref, send_sem, recv_sem, own_sem):
    me = lax.axis_index("row")
    own = feat_ref.shape[0]
    barrier = pltpu.get_barrier_semaphore()
    for k in range(1, n_row):
        peer = lax.rem(me + k, n_row)
        pl.semaphore_signal(barrier, inc=1, device_id={"row": peer}, device_id_type=MESH)
    pl.semaphore_wait(barrier, n_row - 1)
    slot = pl.ds(pl.multiple_of(me * own, own), own)
    copies = []
    for k in range(1, n_row):
        peer = lax.rem(me + k, n_row)
        copy = pltpu.make_async_remote_copy(
            src_ref=feat_ref,
            dst_ref=band_ref.at[slot],
            send_sem=send_sem.at[k],
            recv_sem=recv_sem.at[k],
            device_id={"row": peer},
            device_id_type=MESH,
        )
        copy.start()
        copies.append(copy)
    local_copy = pltpu.make_async_copy(feat_ref, band_ref.at[slot], own_sem)
    local_copy.start()
    fill_zero(total_ref)
    local_copy.wait()
    for k in range(1, n_row):
        src = lax.rem(me - k + n_row, n_row)
        src_slot = pl.ds(pl.multiple_of(src * own, own), own)
        copies[k - 1].wait_send()
        pltpu.make_async_remote_copy(
            src_ref=feat_ref,
            dst_ref=band_ref.at[src_slot],
            send_sem=send_sem.at[k],
            recv_sem=recv_sem.at[k],
            device_id={"row": src},
            device_id_type=MESH,
        ).wait_recv()


def relay_kernel(feat_ref, band_ref, total_ref, send_sem, recv_sem, own_sem):
    me = lax.axis_index("row")
    own = feat_ref.shape[0]
    half = own // 2
    slow, fast = lax.div(me, 2), lax.rem(me, 2)
    peers = (slow * 2 + (1 - fast), (1 - slow) * 2 + fast)
    opposite = (1 - slow) * 2 + (1 - fast)
    barrier = pltpu.get_barrier_semaphore()
    for peer in peers:
        pl.semaphore_signal(barrier, inc=1, device_id={"row": peer}, device_id_type=MESH)
    local_copy = pltpu.make_async_copy(feat_ref, band_ref.at[pl.ds(pl.multiple_of(me * own, own), own)], own_sem)
    local_copy.start()
    pl.semaphore_wait(barrier, 2)

    def span(owner, part):
        return pl.ds(pl.multiple_of(owner * own + part * half, half), half)

    def copy(axis, step, source, owner, part):
        return pltpu.make_async_remote_copy(
            src_ref=source,
            dst_ref=band_ref.at[span(owner, part)],
            send_sem=send_sem.at[axis, step],
            recv_sem=recv_sem.at[axis, step],
            device_id={"row": peers[axis]},
            device_id_type=MESH,
        )

    def own_part(part):
        return feat_ref.at[pl.ds(part * half, half)]

    for step in range(2):
        for axis in range(2):
            part = axis if step == 0 else 1 - axis
            copy(axis, step, own_part(part), me, part).start()
    fill_zero(total_ref)
    for axis in range(2):
        copy(axis, 0, own_part(axis), peers[axis], axis).wait_recv()
        copy(1 - axis, 2, band_ref.at[span(peers[axis], axis)], peers[axis], axis).start()
    local_copy.wait()
    for axis in range(2):
        copy(axis, 1, own_part(0), peers[axis], 1 - axis).wait_recv()
    for axis in range(2):
        copy(axis, 2, own_part(0), opposite, 1 - axis).wait_recv()
    for axis in range(2):
        for step in range(3):
            copy(axis, step, own_part(0), me, 0).wait_send()


def gather(features, n_row, row_blocks):
    own, width = features.shape
    if n_row == 4:
        kernel, sem_shape = relay_kernel, (2, 3)
    else:
        kernel, sem_shape = functools.partial(gather_kernel, n_row), (n_row,)
    return pl.pallas_call(
        kernel,
        out_shape=(
            jax.ShapeDtypeStruct((n_row * own, width), features.dtype),
            jax.ShapeDtypeStruct((row_blocks + 1, BLK, width), jnp.float32),
        ),
        in_specs=[pl.BlockSpec(memory_space=pl.ANY)],
        out_specs=(pl.BlockSpec(memory_space=pltpu.VMEM), pl.BlockSpec(memory_space=pltpu.VMEM)),
        scratch_shapes=[
            pltpu.SemaphoreType.DMA(sem_shape),
            pltpu.SemaphoreType.DMA(sem_shape),
            pltpu.SemaphoreType.DMA,
        ],
        compiler_params=pltpu.CompilerParams(
            collective_id=0, has_side_effects=True, vmem_limit_bytes=16 * 1024 * 1024
        ),
        name="gather_band",
    )(features)


def cell_kernel(slots, index_hbm, band_ref, tiles_ref, zero_ref, acc, index_ref, held, sem, index_sem):
    chunks = slots // CHUNK
    first = min(max(128 // CHUNK, 1), chunks)

    def chunk_copy(i):
        part = pl.ds(i * CHUNK, CHUNK)
        return pltpu.make_async_copy(tiles_ref.at[part], held.at[part], sem.at[i])

    index_copy = pltpu.make_async_copy(index_hbm, index_ref, index_sem)
    index_copy.start()
    for i in range(first):
        chunk_copy(i).start()
    index_copy.wait()
    count = index_ref[slots]
    for i in range(first, chunks):
        @pl.when(i * CHUNK < count)
        def _():
            chunk_copy(i).start()

    def chunk_step(i, carry):
        chunk_copy(i).wait()
        for u in range(CHUNK):
            t = i * CHUNK + u
            index = index_ref[t]
            block = band_ref[index & 0xFFFF]
            acc[index >> 16] += jnp.dot(held[t], block, preferred_element_type=jnp.float32)
        return carry

    lax.fori_loop(0, jnp.maximum(lax.div(count + CHUNK - 1, CHUNK), first), chunk_step, 0)


def cell_partial(rows, cols, count, band, tiles, zero):
    slots = tiles.shape[0]
    width = band.shape[1]
    col_blocks = band.shape[0] // BLK
    row_blocks = zero.shape[0] - 1
    live_rows = jnp.where(jnp.arange(slots, dtype=jnp.int32) < count, rows, row_blocks)
    index = jnp.concatenate([live_rows * 65536 + cols, jnp.broadcast_to(count, (BLK,))])
    hbm = pl.BlockSpec(memory_space=pl.ANY)
    vmem = pl.BlockSpec(memory_space=pltpu.VMEM)
    return pl.pallas_call(
        functools.partial(cell_kernel, slots),
        out_shape=jax.ShapeDtypeStruct(zero.shape, zero.dtype),
        in_specs=[hbm, vmem, hbm, vmem],
        out_specs=vmem,
        scratch_shapes=[
            pltpu.SMEM((slots + BLK,), jnp.int32),
            pltpu.VMEM((slots, BLK, BLK), jnp.bfloat16),
            pltpu.SemaphoreType.DMA((slots // CHUNK,)),
            pltpu.SemaphoreType.DMA,
        ],
        input_output_aliases={3: 0},
        compiler_params=pltpu.CompilerParams(vmem_limit_bytes=48 * 1024 * 1024),
        cost_estimate=pl.CostEstimate(
            flops=2 * slots * BLK * BLK * width, bytes_accessed=slots * BLK * BLK * 2, transcendentals=0
        ),
        name="cell_partial",
    )(index, band.reshape(col_blocks, BLK, width), tiles, zero)


def reduce_kernel(
    line, own, part_ref, weight_ref, bias_ref, out_ref,
    pair_out, pair_buf, up_in, down_in, up_out, down_out,
    pair_send, pair_recv, up_send, up_recv, down_send, down_recv,
):
    col = lax.axis_index("col")
    chip = lax.div(col, 2)
    core = lax.rem(col, 2)
    other = 1 - core
    rows = own // PIECES
    f32 = jnp.float32
    has_low = chip > 0
    has_high = chip < line - 1
    partner = chip * 2 + other
    high = lax.rem(col + 2, 2 * line)
    low = lax.rem(col - 2 + 2 * line, 2 * line)

    barrier = pltpu.get_barrier_semaphore()
    pl.semaphore_signal(barrier, inc=1, device_id={"col": partner}, device_id_type=MESH)

    @pl.when(has_low)
    def _():
        pl.semaphore_signal(barrier, inc=1, device_id={"col": low}, device_id_type=MESH)

    @pl.when(has_high)
    def _():
        pl.semaphore_signal(barrier, inc=1, device_id={"col": high}, device_id_type=MESH)

    pl.semaphore_wait(barrier, 1 + jnp.where(has_low, 1, 0) + jnp.where(has_high, 1, 0))

    def pair_copy(dest, piece):
        span = pl.ds(piece * rows, rows)
        return pltpu.make_async_remote_copy(
            src_ref=pair_out.at[dest, span],
            dst_ref=pair_buf.at[dest, span],
            send_sem=pair_send.at[dest, piece],
            recv_sem=pair_recv.at[dest, piece],
            device_id={"col": partner},
            device_id_type=MESH,
        )

    def pair_start(dest):
        for piece in range(PIECES):
            theirs = pl.ds(pl.multiple_of((dest * 2 + other) * own + piece * rows, rows), rows)
            pair_out[dest, pl.ds(piece * rows, rows), :] = part_ref[theirs, :].astype(pair_out.dtype)
            pair_copy(dest, piece).start()

    def line_copy(dest, piece, upward):
        span = pl.ds(piece * rows, rows)
        src, dst = (up_out, up_in) if upward else (down_out, down_in)
        send, recv = (up_send, up_recv) if upward else (down_send, down_recv)
        return pltpu.make_async_remote_copy(
            src_ref=src.at[dest, span],
            dst_ref=dst.at[dest, span],
            send_sem=send.at[dest, piece],
            recv_sem=recv.at[dest, piece],
            device_id={"col": high if upward else low},
            device_id_type=MESH,
        )

    def pair_sum(dest, piece):
        mine = pl.ds(pl.multiple_of((dest * 2 + core) * own + piece * rows, rows), rows)
        span = pl.ds(piece * rows, rows)
        return part_ref[mine, :] + pair_buf[dest, span, :].astype(f32)

    for dist in range(line - 1, 0, -1):
        @pl.when(chip + dist < line)
        def _():
            pair_start(chip + dist)

        @pl.when(chip - dist >= 0)
        def _():
            pair_start(chip - dist)

    pair_start(chip)

    def forward(dest, piece, upward):
        pair_copy(dest, piece).wait_recv()
        from_line = has_low if upward else has_high
        buf = up_in if upward else down_in
        out = up_out if upward else down_out
        span = pl.ds(piece * rows, rows)

        @pl.when(from_line)
        def _():
            line_copy(dest, piece, upward).wait_recv()
            out[dest, span, :] = (pair_sum(dest, piece) + buf[dest, span, :].astype(f32)).astype(out.dtype)

        @pl.when(jnp.logical_not(from_line))
        def _():
            out[dest, span, :] = pair_sum(dest, piece).astype(out.dtype)

        line_copy(dest, piece, upward).start()

    for dist in range(line - 1, 0, -1):
        for piece in range(PIECES):
            @pl.when(chip + dist < line)
            def _():
                forward(chip + dist, piece, True)

            @pl.when(chip - dist >= 0)
            def _():
                forward(chip - dist, piece, False)

    for piece in range(PIECES):
        span = pl.ds(piece * rows, rows)
        pair_copy(chip, piece).wait_recv()

        @pl.when(has_low)
        def _():
            line_copy(chip, piece, True).wait_recv()

        @pl.when(has_high)
        def _():
            line_copy(chip, piece, False).wait_recv()

        total = pair_sum(chip, piece)
        total = total + jnp.where(has_low, up_in[chip, span, :].astype(f32), 0.0)
        total = total + jnp.where(has_high, down_in[chip, span, :].astype(f32), 0.0)
        mixed = jnp.dot(total.astype(jnp.bfloat16), weight_ref[...], preferred_element_type=f32)
        out_ref[span, :] = jnp.maximum(mixed + bias_ref[...], 0.0).astype(out_ref.dtype)

    for dest in range(line):
        for piece in range(PIECES):
            pair_copy(dest, piece).wait_send()

            @pl.when(chip < dest)
            def _():
                line_copy(dest, piece, True).wait_send()

            @pl.when(chip > dest)
            def _():
                line_copy(dest, piece, False).wait_send()


def reduce_mix(partial_value, weight, bias, n_col, own):
    width = partial_value.shape[1]
    line = n_col // 2
    vmem = pl.BlockSpec(memory_space=pltpu.VMEM)
    buf = pltpu.VMEM((line, own, width), jnp.bfloat16)
    sems = pltpu.SemaphoreType.DMA((line, PIECES))
    return pl.pallas_call(
        functools.partial(reduce_kernel, line, own),
        out_shape=jax.ShapeDtypeStruct((own, width), jnp.bfloat16),
        in_specs=[vmem, vmem, vmem],
        out_specs=vmem,
        scratch_shapes=[buf] * 6 + [sems] * 6,
        compiler_params=pltpu.CompilerParams(
            collective_id=1, has_side_effects=True, vmem_limit_bytes=32 * 1024 * 1024
        ),
        name="reduce_mix",
    )(partial_value, weight, bias)


def local(n_row, n_col, features, tiles, tile_rows, tile_cols, tile_counts, weight, bias):
    own, width = features.shape
    slots = tiles.shape[2]
    row_blocks = n_col * own // BLK
    band, zero = gather(features, n_row, row_blocks)
    partial_value = cell_partial(
        tile_rows.reshape(slots),
        tile_cols.reshape(slots),
        tile_counts.reshape(1),
        band,
        tiles.reshape(slots, BLK, BLK),
        zero,
    )
    return reduce_mix(
        partial_value.reshape((row_blocks + 1) * BLK, width), weight, bias.reshape(1, width), n_col, own
    )


def solution(mesh):
    in_specs = (
        P(("col", "row"), None),
        P("row", "col", None, None, None),
        P("row", "col", None),
        P("row", "col", None),
        P("row", "col"),
        P(),
        P(),
    )
    out_specs = P(("row", "col"), None)
    fn = functools.partial(local, mesh.shape["row"], mesh.shape["col"])
    return jax.shard_map(fn, mesh=mesh, in_specs=in_specs, out_specs=out_specs, check_vma=False)
```

```python
import functools

import jax
import jax.numpy as jnp
from jax import lax
from jax.experimental import pallas as pl
from jax.experimental.pallas import tpu as pltpu
from jax.sharding import PartitionSpec as P

MESH = pl.DeviceIdType.MESH
BLK = 128
CHUNK = 64
PIECES = 4


def fill_zero(total_ref):
    def fill(i, carry):
        total_ref[i] = jnp.zeros(total_ref.shape[1:], total_ref.dtype)
        return carry

    lax.fori_loop(0, total_ref.shape[0], fill, 0)


def gather_kernel(n_row, feat_ref, band_ref, total_ref, send_sem, recv_sem, own_sem):
    me = lax.axis_index("row")
    own = feat_ref.shape[0]
    barrier = pltpu.get_barrier_semaphore()
    for k in range(1, n_row):
        peer = lax.rem(me + k, n_row)
        pl.semaphore_signal(barrier, inc=1, device_id={"row": peer}, device_id_type=MESH)
    pl.semaphore_wait(barrier, n_row - 1)
    slot = pl.ds(pl.multiple_of(me * own, own), own)
    copies = []
    for k in range(1, n_row):
        peer = lax.rem(me + k, n_row)
        copy = pltpu.make_async_remote_copy(
            src_ref=feat_ref,
            dst_ref=band_ref.at[slot],
            send_sem=send_sem.at[k],
            recv_sem=recv_sem.at[k],
            device_id={"row": peer},
            device_id_type=MESH,
        )
        copy.start()
        copies.append(copy)
    local_copy = pltpu.make_async_copy(feat_ref, band_ref.at[slot], own_sem)
    local_copy.start()
    fill_zero(total_ref)
    local_copy.wait()
    for k in range(1, n_row):
        src = lax.rem(me - k + n_row, n_row)
        src_slot = pl.ds(pl.multiple_of(src * own, own), own)
        copies[k - 1].wait_send()
        pltpu.make_async_remote_copy(
            src_ref=feat_ref,
            dst_ref=band_ref.at[src_slot],
            send_sem=send_sem.at[k],
            recv_sem=recv_sem.at[k],
            device_id={"row": src},
            device_id_type=MESH,
        ).wait_recv()


def relay_kernel(feat_ref, band_ref, total_ref, send_sem, recv_sem, own_sem):
    me = lax.axis_index("row")
    own = feat_ref.shape[0]
    half = own // 2
    slow, fast = lax.div(me, 2), lax.rem(me, 2)
    peers = (slow * 2 + (1 - fast), (1 - slow) * 2 + fast)
    opposite = (1 - slow) * 2 + (1 - fast)
    barrier = pltpu.get_barrier_semaphore()
    for peer in peers:
        pl.semaphore_signal(barrier, inc=1, device_id={"row": peer}, device_id_type=MESH)
    local_copy = pltpu.make_async_copy(feat_ref, band_ref.at[pl.ds(pl.multiple_of(me * own, own), own)], own_sem)
    local_copy.start()
    pl.semaphore_wait(barrier, 2)

    def span(owner, part):
        return pl.ds(pl.multiple_of(owner * own + part * half, half), half)

    def copy(axis, step, source, owner, part):
        return pltpu.make_async_remote_copy(
            src_ref=source,
            dst_ref=band_ref.at[span(owner, part)],
            send_sem=send_sem.at[axis, step],
            recv_sem=recv_sem.at[axis, step],
            device_id={"row": peers[axis]},
            device_id_type=MESH,
        )

    def own_part(part):
        return feat_ref.at[pl.ds(part * half, half)]

    for step in range(2):
        for axis in range(2):
            part = axis if step == 0 else 1 - axis
            copy(axis, step, own_part(part), me, part).start()
    fill_zero(total_ref)
    for axis in range(2):
        copy(axis, 0, own_part(axis), peers[axis], axis).wait_recv()
        copy(1 - axis, 2, band_ref.at[span(peers[axis], axis)], peers[axis], axis).start()
    local_copy.wait()
    for axis in range(2):
        copy(axis, 1, own_part(0), peers[axis], 1 - axis).wait_recv()
    for axis in range(2):
        copy(axis, 2, own_part(0), opposite, 1 - axis).wait_recv()
    for axis in range(2):
        for step in range(3):
            copy(axis, step, own_part(0), me, 0).wait_send()


def gather(features, n_row, row_blocks):
    own, width = features.shape
    if n_row == 4:
        kernel, sem_shape = relay_kernel, (2, 3)
    else:
        kernel, sem_shape = functools.partial(gather_kernel, n_row), (n_row,)
    return pl.pallas_call(
        kernel,
        out_shape=(
            jax.ShapeDtypeStruct((n_row * own, width), features.dtype),
            jax.ShapeDtypeStruct((row_blocks + 1, BLK, width), jnp.float32),
        ),
        in_specs=[pl.BlockSpec(memory_space=pl.ANY)],
        out_specs=(pl.BlockSpec(memory_space=pltpu.VMEM), pl.BlockSpec(memory_space=pltpu.VMEM)),
        scratch_shapes=[
            pltpu.SemaphoreType.DMA(sem_shape),
            pltpu.SemaphoreType.DMA(sem_shape),
            pltpu.SemaphoreType.DMA,
        ],
        compiler_params=pltpu.CompilerParams(
            collective_id=0, has_side_effects=True, vmem_limit_bytes=16 * 1024 * 1024
        ),
        name="gather_band",
    )(features)


def cell_kernel(slots, index_hbm, band_ref, tiles_ref, zero_ref, acc, index_ref, held, sem, index_sem):
    chunks = slots // CHUNK
    first = min(max(128 // CHUNK, 1), chunks)

    def chunk_copy(i):
        part = pl.ds(i * CHUNK, CHUNK)
        return pltpu.make_async_copy(tiles_ref.at[part], held.at[part], sem.at[i])

    index_copy = pltpu.make_async_copy(index_hbm, index_ref, index_sem)
    index_copy.start()
    for i in range(first):
        chunk_copy(i).start()
    index_copy.wait()
    count = index_ref[slots]
    for i in range(first, chunks):
        @pl.when(i * CHUNK < count)
        def _():
            chunk_copy(i).start()

    def chunk_step(i, carry):
        chunk_copy(i).wait()
        for u in range(CHUNK):
            t = i * CHUNK + u
            index = index_ref[t]
            block = band_ref[index & 0xFFFF]
            acc[index >> 16] += jnp.dot(held[t], block, preferred_element_type=jnp.float32)
        return carry

    lax.fori_loop(0, jnp.maximum(lax.div(count + CHUNK - 1, CHUNK), first), chunk_step, 0)


def cell_partial(rows, cols, count, band, tiles, zero):
    slots = tiles.shape[0]
    width = band.shape[1]
    col_blocks = band.shape[0] // BLK
    row_blocks = zero.shape[0] - 1
    live_rows = jnp.where(jnp.arange(slots, dtype=jnp.int32) < count, rows, row_blocks)
    index = jnp.concatenate([live_rows * 65536 + cols, jnp.broadcast_to(count, (BLK,))])
    hbm = pl.BlockSpec(memory_space=pl.ANY)
    vmem = pl.BlockSpec(memory_space=pltpu.VMEM)
    return pl.pallas_call(
        functools.partial(cell_kernel, slots),
        out_shape=jax.ShapeDtypeStruct(zero.shape, zero.dtype),
        in_specs=[hbm, vmem, hbm, vmem],
        out_specs=vmem,
        scratch_shapes=[
            pltpu.SMEM((slots + BLK,), jnp.int32),
            pltpu.VMEM((slots, BLK, BLK), jnp.bfloat16),
            pltpu.SemaphoreType.DMA((slots // CHUNK,)),
            pltpu.SemaphoreType.DMA,
        ],
        input_output_aliases={3: 0},
        compiler_params=pltpu.CompilerParams(vmem_limit_bytes=48 * 1024 * 1024),
        cost_estimate=pl.CostEstimate(
            flops=2 * slots * BLK * BLK * width, bytes_accessed=slots * BLK * BLK * 2, transcendentals=0
        ),
        name="cell_partial",
    )(index, band.reshape(col_blocks, BLK, width), tiles, zero)


def reduce_kernel(
    line, own, part_ref, weight_ref, bias_ref, out_ref,
    pair_out, pair_buf, up_in, down_in, up_out, down_out,
    pair_send, pair_recv, up_send, up_recv, down_send, down_recv,
):
    col = lax.axis_index("col")
    chip = lax.div(col, 2)
    core = lax.rem(col, 2)
    other = 1 - core
    rows = own // PIECES
    f32 = jnp.float32
    has_low = chip > 0
    has_high = chip < line - 1
    partner = chip * 2 + other
    high = lax.rem(col + 2, 2 * line)
    low = lax.rem(col - 2 + 2 * line, 2 * line)

    barrier = pltpu.get_barrier_semaphore()
    pl.semaphore_signal(barrier, inc=1, device_id={"col": partner}, device_id_type=MESH)

    @pl.when(has_low)
    def _():
        pl.semaphore_signal(barrier, inc=1, device_id={"col": low}, device_id_type=MESH)

    @pl.when(has_high)
    def _():
        pl.semaphore_signal(barrier, inc=1, device_id={"col": high}, device_id_type=MESH)

    pl.semaphore_wait(barrier, 1 + jnp.where(has_low, 1, 0) + jnp.where(has_high, 1, 0))

    def pair_copy(dest, piece):
        span = pl.ds(piece * rows, rows)
        return pltpu.make_async_remote_copy(
            src_ref=pair_out.at[dest, span],
            dst_ref=pair_buf.at[dest, span],
            send_sem=pair_send.at[dest, piece],
            recv_sem=pair_recv.at[dest, piece],
            device_id={"col": partner},
            device_id_type=MESH,
        )

    def pair_start(dest):
        for piece in range(PIECES):
            theirs = pl.ds(pl.multiple_of((dest * 2 + other) * own + piece * rows, rows), rows)
            pair_out[dest, pl.ds(piece * rows, rows), :] = part_ref[theirs, :].astype(pair_out.dtype)
            pair_copy(dest, piece).start()

    def line_copy(dest, piece, upward):
        span = pl.ds(piece * rows, rows)
        src, dst = (up_out, up_in) if upward else (down_out, down_in)
        send, recv = (up_send, up_recv) if upward else (down_send, down_recv)
        return pltpu.make_async_remote_copy(
            src_ref=src.at[dest, span],
            dst_ref=dst.at[dest, span],
            send_sem=send.at[dest, piece],
            recv_sem=recv.at[dest, piece],
            device_id={"col": high if upward else low},
            device_id_type=MESH,
        )

    def pair_sum(dest, piece):
        mine = pl.ds(pl.multiple_of((dest * 2 + core) * own + piece * rows, rows), rows)
        span = pl.ds(piece * rows, rows)
        return part_ref[mine, :] + pair_buf[dest, span, :].astype(f32)

    def pair_start_at(dist):
        if dist == 0:
            pair_start(chip)
            return

        @pl.when(chip + dist < line)
        def _():
            pair_start(chip + dist)

        @pl.when(chip - dist >= 0)
        def _():
            pair_start(chip - dist)

    pair_start_at(line - 1)

    def forward(dest, piece, upward):
        pair_copy(dest, piece).wait_recv()
        from_line = has_low if upward else has_high
        buf = up_in if upward else down_in
        out = up_out if upward else down_out
        span = pl.ds(piece * rows, rows)

        @pl.when(from_line)
        def _():
            line_copy(dest, piece, upward).wait_recv()
            out[dest, span, :] = (pair_sum(dest, piece) + buf[dest, span, :].astype(f32)).astype(out.dtype)

        @pl.when(jnp.logical_not(from_line))
        def _():
            out[dest, span, :] = pair_sum(dest, piece).astype(out.dtype)

        line_copy(dest, piece, upward).start()

    for dist in range(line - 1, 0, -1):
        for piece in range(PIECES):
            @pl.when(chip + dist < line)
            def _():
                forward(chip + dist, piece, True)

            @pl.when(chip - dist >= 0)
            def _():
                forward(chip - dist, piece, False)

            if piece == 0:
                pair_start_at(dist - 1)

    for piece in range(PIECES):
        span = pl.ds(piece * rows, rows)
        pair_copy(chip, piece).wait_recv()

        @pl.when(has_low)
        def _():
            line_copy(chip, piece, True).wait_recv()

        @pl.when(has_high)
        def _():
            line_copy(chip, piece, False).wait_recv()

        total = pair_sum(chip, piece)
        total = total + jnp.where(has_low, up_in[chip, span, :].astype(f32), 0.0)
        total = total + jnp.where(has_high, down_in[chip, span, :].astype(f32), 0.0)
        mixed = jnp.dot(total.astype(jnp.bfloat16), weight_ref[...], preferred_element_type=f32)
        out_ref[span, :] = jnp.maximum(mixed + bias_ref[...], 0.0).astype(out_ref.dtype)

    for dest in range(line):
        for piece in range(PIECES):
            pair_copy(dest, piece).wait_send()

            @pl.when(chip < dest)
            def _():
                line_copy(dest, piece, True).wait_send()

            @pl.when(chip > dest)
            def _():
                line_copy(dest, piece, False).wait_send()


def reduce_mix(partial_value, weight, bias, n_col, own):
    width = partial_value.shape[1]
    line = n_col // 2
    vmem = pl.BlockSpec(memory_space=pltpu.VMEM)
    buf = pltpu.VMEM((line, own, width), jnp.bfloat16)
    sems = pltpu.SemaphoreType.DMA((line, PIECES))
    return pl.pallas_call(
        functools.partial(reduce_kernel, line, own),
        out_shape=jax.ShapeDtypeStruct((own, width), jnp.bfloat16),
        in_specs=[vmem, vmem, vmem],
        out_specs=vmem,
        scratch_shapes=[buf] * 6 + [sems] * 6,
        compiler_params=pltpu.CompilerParams(
            collective_id=1, has_side_effects=True, vmem_limit_bytes=32 * 1024 * 1024
        ),
        name="reduce_mix",
    )(partial_value, weight, bias)


def local(n_row, n_col, features, tiles, tile_rows, tile_cols, tile_counts, weight, bias):
    own, width = features.shape
    slots = tiles.shape[2]
    row_blocks = n_col * own // BLK
    band, zero = gather(features, n_row, row_blocks)
    partial_value = cell_partial(
        tile_rows.reshape(slots),
        tile_cols.reshape(slots),
        tile_counts.reshape(1),
        band,
        tiles.reshape(slots, BLK, BLK),
        zero,
    )
    return reduce_mix(
        partial_value.reshape((row_blocks + 1) * BLK, width), weight, bias.reshape(1, width), n_col, own
    )


def solution(mesh):
    in_specs = (
        P(("col", "row"), None),
        P("row", "col", None, None, None),
        P("row", "col", None),
        P("row", "col", None),
        P("row", "col"),
        P(),
        P(),
    )
    out_specs = P(("row", "col"), None)
    fn = functools.partial(local, mesh.shape["row"], mesh.shape["col"])
    return jax.shard_map(fn, mesh=mesh, in_specs=in_specs, out_specs=out_specs, check_vma=False)
```
